32 devices in a mesh: ctx: 16 (over z, y, x), head: 2 (over core).
Axes of the slice: x: 2, y: 2, z: 4, core: 2. Of those that a mesh axis runs over, the one named last changes fastest.
Arguments:
- queries: bfloat16 [8192, 4096], P('ctx', 'head'), may hold values from -6 to 6
- keys: bfloat16 [8192, 4096], P('ctx', 'head'), may hold values from -6 to 6
- values: bfloat16 [8192, 4096], P('ctx', 'head'), may hold values from -6 to 6
- doc_start: int32 [32], P('ctx'), may hold values from 0 to 256, as said below
- decay_rate: float32 [32], P('head'), may hold values from 3.6621094e-05 to 0.032552083
- gain: float32 [4096], P('head'), may hold values from 0.25 to 1.75
- plan_offset: int32 [16], replicated, may hold values from 0 to 1, as said below
Outputs:
- mixed: bfloat16 [12288, 4096], P('ctx', 'head')
The draws below stay inside these ranges and needn't reach their ends.
Inputs may be any that keep to these rules, and one draw needn't show every extreme that they name: `doc_start`: at most one document begins in a block. plan_offset[0] is 0 and every other entry is 0 or 1; some shard takes 2 * 2 - 1 blocks.
All inputs are finite; a program needn't handle non-finite values.
Results may differ from the reference program's by a relative error of at most 0.0011.
The reference program's roundings to bfloat16 on the way count: a program that leaves them out, or rounds other values in their place, can miss the bound.
Values may be sent and summed in bfloat16 or wider, within the bound.
A program may use at most 128 MiB of HBM per device.

```python
import math
from functools import partial
import jax
import jax.numpy as jnp
from jax import lax

HD = 128
HEADS = 32
BLOCK = 256
BLK_DEV = 2
NBLK = 32
TOKENS = 8192
WIDTH = 4096
SLOTS = 3
OUT_ROWS = 12288
N_CTX = 16


def draw_decay_rate(key, part):
    key_one, key_two, key_three = jax.random.split(key, 3)
    fraction = 0.5
    quick = jax.random.uniform(key_one, (HEADS,)) < fraction
    quick_rate = jnp.exp(jax.random.uniform(key_two, (HEADS,), minval=math.log(1.0 / (0.2 * BLOCK)), maxval=math.log(1.0 / (0.12 * BLOCK))))
    slow_rate = jnp.exp(jax.random.uniform(key_three, (HEADS,), minval=math.log(0.3 / TOKENS), maxval=math.log(2.0 / TOKENS)))
    return jnp.where(quick, quick_rate, slow_rate).astype(jnp.float32)


def draw_doc_start(key, part):
    key_one, key_two, key_three = jax.random.split(key, 3)
    chosen = jax.random.randint(key_one, (NBLK,), 0, 6)
    position = jax.random.randint(key_two, (NBLK,), 0, BLOCK)
    stretch = NBLK // 2
    quiet_first = jax.random.randint(key_three, (), 0, NBLK - stretch + 1)
    blocks = jnp.arange(NBLK, dtype=jnp.int32)
    quiet = (blocks >= quiet_first) & (blocks < quiet_first + stretch)
    starting = (chosen == 0) & jnp.logical_not(quiet)
    return jnp.where(starting, position, BLOCK).astype(jnp.int32)


def draw_plan_offset(key, part):
    shards = NBLK // BLK_DEV
    offsets = jax.random.randint(key, (shards,), 1, BLK_DEV)
    places = jnp.arange(shards, dtype=jnp.int32)
    offsets = jnp.where(places == 1, BLK_DEV - 1, offsets)
    offsets = jnp.where(places == 0, 0, offsets)
    return offsets.astype(jnp.int32)


def block_levels(rng, extent, cuts, smallest, high):
    def one(axis_at, shards_of):
        steps = jax.random.uniform(jax.random.fold_in(jax.random.fold_in(rng, 6), axis_at), (shards_of,), jnp.float32, smallest / len(cuts), high / len(cuts))
        return jnp.repeat(jnp.exp(steps), extent[axis_at] // shards_of).reshape((-1,) + (1,) * (len(extent) - axis_at - 1))

    level = one(*cuts[0])
    for cut in cuts[1:]:
        level = level * one(*cut)
    return level


def gaussian(rng, dims, deviation, most, cuts=(), held_as=jnp.bfloat16):
    values = deviation * jax.random.normal(rng, dims, jnp.float32)
    if cuts:
        values = values * block_levels(rng, dims, cuts, -0.22, 0.18)
    return jnp.clip(values, -most, most).astype(held_as)


def setup_inputs(seed: int = 0) -> dict:
    splits = jax.random.split(jax.random.key(seed), 8)
    queries = gaussian(splits[0], (TOKENS, WIDTH), 1.0, 6.0, ((0, 16), (1, 2)))
    keys = gaussian(splits[1], (TOKENS, WIDTH), 1.0, 6.0, ((0, 16), (1, 2)))
    values = gaussian(splits[2], (TOKENS, WIDTH), 1.0, 6.0, ((0, 16), (1, 2)))
    doc_start = draw_doc_start(jax.random.fold_in(splits[7], 71), 0)
    decay_rate = draw_decay_rate(jax.random.fold_in(splits[7], 71), 0)
    gain = jnp.clip(1.0 + 0.15 * jax.random.normal(splits[5], (WIDTH,), jnp.float32), 0.25, 1.75)
    plan_offset = draw_plan_offset(jax.random.fold_in(splits[7], 71), 0)
    return dict(queries=queries, keys=keys, values=values, doc_start=doc_start, decay_rate=decay_rate, gain=gain, plan_offset=plan_offset)


EPSILON = 1e-06

def head_pass(doc_start, operands):
    q_blocks, k_blocks, v_blocks, rate = operands
    position = jnp.arange(BLOCK, dtype=jnp.int32)
    place_float = position.astype(jnp.float32)
    distance = place_float[:, None] - place_float[None, :]
    weights = jnp.where(distance >= 0, jnp.exp(-rate * jnp.maximum(distance, 0.0)), 0.0)
    marks = doc_start[:, None, None]
    allowed = jnp.logical_not((position[None, None, :] < marks) & (marks <= position[None, :, None])).astype(jnp.float32)
    scores = jnp.einsum('bid,bjd->bij', q_blocks.astype(jnp.float32), k_blocks.astype(jnp.float32))
    probs = (scores * weights[None] * allowed).astype(jnp.bfloat16)
    intra = jnp.einsum('bij,bjd->bid', probs.astype(jnp.float32), v_blocks.astype(jnp.float32))
    key_keep = (position[None, :] >= doc_start[:, None]).astype(jnp.float32)
    key_decay = jnp.exp(-rate * (BLOCK - 1 - place_float))
    weighted = (k_blocks.astype(jnp.float32) * key_decay[None, :, None] * key_keep[:, :, None]).astype(jnp.bfloat16)
    updates = jnp.einsum('bjd,bje->bde', weighted.astype(jnp.float32), v_blocks.astype(jnp.float32))
    carry = jnp.where(doc_start == BLOCK, jnp.exp(-rate * BLOCK), 0.0)

    def advance(state_now, pair_in):
        decay_now, update_now = pair_in
        return (decay_now * state_now + update_now, state_now)
    _, states = lax.scan(advance, jnp.zeros((HD, HD), jnp.float32), (carry, updates))
    query_keep = (position[None, :] < doc_start[:, None]).astype(jnp.float32)
    query_decay = jnp.exp(-rate * (place_float + 1.0))[None, :] * query_keep
    inter = jnp.einsum('bid,bde->bie', q_blocks.astype(jnp.float32), states, precision=lax.Precision.HIGHEST)
    return intra + inter * query_decay[:, :, None]

def reference(queries, keys, values, doc_start, decay_rate, gain, plan_offset):
    shaped = (NBLK, BLOCK, HEADS, HD)

    def per_head(array):
        return array.reshape(shaped).transpose(2, 0, 1, 3)
    attended = lax.map(partial(head_pass, doc_start), (per_head(queries), per_head(keys), per_head(values), decay_rate))
    attended = attended.transpose(1, 2, 0, 3).reshape(TOKENS, WIDTH)
    squares = lax.optimization_barrier(jnp.sum(attended * attended, axis=1))
    scaling = lax.rsqrt(squares / WIDTH + EPSILON)
    normed = (attended * scaling[:, None] * gain[None, :]).astype(jnp.bfloat16)
    blocks = normed.reshape(NBLK, BLOCK, WIDTH)
    shard_ids = jnp.arange(N_CTX, dtype=jnp.int32)
    following = jnp.concatenate([plan_offset[1:], jnp.zeros((1,), jnp.int32)])
    first_block = shard_ids * BLK_DEV + plan_offset
    lengths = BLK_DEV + following - plan_offset
    slot_ids = jnp.arange(SLOTS, dtype=jnp.int32)
    picked = jnp.clip(first_block[:, None] + slot_ids[None, :], 0, NBLK - 1).astype(jnp.int32)
    live = (slot_ids[None, :] < lengths[:, None]).reshape(-1)
    chosen = jnp.take(blocks, picked.reshape(-1), axis=0)
    chosen = jnp.where(live[:, None, None], chosen, jnp.zeros((), jnp.bfloat16))
    return chosen.reshape(OUT_ROWS, WIDTH)
```

```python
import functools

import jax
import jax.numpy as jnp
from jax import lax
from jax.experimental import pallas as pl
from jax.experimental.pallas import tpu as pltpu
from jax.sharding import PartitionSpec as P

HD = 128
BLOCK = 256
GROUP = 4
EPSILON = 1e-06
F32 = jnp.float32
BF16 = jnp.bfloat16
CHUNKS = 4
CROWS = BLOCK // CHUNKS


def dot(a, b, dims):
    return lax.dot_general(a, b, (dims, ((), ())), preferred_element_type=F32)


def kernel(
    n, hn, heads, width,
    start_ref, rate_ref, plan_ref, q_ref, k_ref, v_ref, gain_ref,
    out_ref,
    att, u0, mask, dist, sbuf, p1, pre, chain_in, chain_out, p3out, p3,
    ssq, ssq_in, halo_out, own1, halo_in,
    p1_send, p1_recv, ch_send, ch_recv, p3_send, p3_recv, sq_send, sq_recv, ha_send, ha_recv,
):
    hq = heads // GROUP
    zs = n // GROUP
    p = lax.axis_index("ctx")
    me = lax.axis_index("head")
    g = p // GROUP
    r = p % GROUP
    base = g * GROUP

    barrier = pltpu.get_barrier_semaphore()

    def greet(ctx, head):
        pl.semaphore_signal(
            barrier, inc=1, device_id=(ctx, head), device_id_type=pl.DeviceIdType.MESH
        )

    for t in range(1, GROUP):
        greet(base + (r + t) % GROUP, me)
    for t in range(1, hn):
        greet(p, (me + t) % hn)
    pl.when(g > 0)(lambda: greet(p - GROUP, me))
    pl.when(g < zs - 1)(lambda: greet(p + GROUP, me))
    pl.when(p > 0)(lambda: greet(p - 1, me))
    pl.when(p < n - 1)(lambda: greet(p + 1, me))

    start = [start_ref[0], start_ref[1]]
    flag = [jnp.where(s == BLOCK, 1.0, 0.0).astype(F32) for s in start]

    def cols(h):
        return pl.ds(pl.multiple_of(h * HD, HD), HD)

    def rows(b):
        return pl.ds(b * BLOCK, BLOCK)

    def power(h, count):
        return jnp.exp(jnp.full((1, HD), -rate_ref[h] * count, F32))

    def remote(src, dst, send, recv, ctx, head):
        return pltpu.make_async_remote_copy(
            src_ref=src, dst_ref=dst, send_sem=send, recv_sem=recv,
            device_id=(ctx, head), device_id_type=pl.DeviceIdType.MESH,
        )

    place = lax.broadcasted_iota(jnp.int32, (BLOCK, HD), 0)
    place_f = place.astype(F32)

    def shard_state(h):
        decay = jnp.exp(-rate_ref[h] * (BLOCK - 1 - place_f))
        parts = []
        for b in range(2):
            keys = k_ref[rows(b), cols(h)].astype(F32) * decay
            weighted = jnp.where(place >= start[b], keys, 0.0).astype(BF16)
            parts.append(dot(weighted, v_ref[rows(b), cols(h)], ((0,), (0,))))
        u0[h] = parts[0]
        return (flag[1] * power(h, float(BLOCK))) * parts[0] + parts[1]

    both = jnp.full((8, HD), flag[0] * flag[1], F32)

    def p1_copy(c, t):
        to = (r + t) % GROUP
        return remote(sbuf.at[c, t - 1], p1.at[c, r], p1_send.at[c, t - 1], p1_recv.at[c, r], base + to, me)

    def p1_arrival(c, t):
        src = (r + t) % GROUP
        return remote(sbuf.at[c, t - 1], p1.at[c, src], p1_send.at[c, t - 1], p1_recv.at[c, src], base + src, me)

    def first(c, carry):
        for t in (1, 2, 3):
            to = (r + t) % GROUP
            sbuf[c, t - 1, 0:HD] = shard_state(to * hq + c)
            sbuf[c, t - 1, HD:HD + 8] = both
        p1[c, r, 0:HD] = shard_state(r * hq + c)
        p1[c, r, HD:HD + 8] = both

        @pl.when(c == 0)
        def _():
            expected = GROUP - 1 + hn - 1
            expected = expected + jnp.where(g > 0, 1, 0) + jnp.where(g < zs - 1, 1, 0)
            expected = expected + jnp.where(p > 0, 1, 0) + jnp.where(p < n - 1, 1, 0)
            pl.semaphore_wait(barrier, expected)

        for t in (1, 2, 3):
            p1_copy(c, t).start()
        return carry

    lax.fori_loop(0, hq, first, 0)

    i_at = lax.broadcasted_iota(jnp.int32, (BLOCK, BLOCK), 0)
    j_at = lax.broadcasted_iota(jnp.int32, (BLOCK, BLOCK), 1)
    apart = i_at - j_at
    dist[...] = jnp.maximum(apart, 0).astype(F32)
    for b in range(2):
        blocked = (j_at < start[b]) & (start[b] <= i_at)
        mask[b] = jnp.where(blocked, 0.0, jnp.where(apart >= 0, 1.0, 0.0))

    per = 2

    def intra(step, carry):
        for s in range(per):
            h = step * per + s
            weights = jnp.exp(-rate_ref[h] * dist[...])
            for b in range(2):
                scores = dot(q_ref[rows(b), cols(h)], k_ref[rows(b), cols(h)], ((1,), (1,)))
                probs = (scores * weights * mask[b]).astype(BF16)
                att[rows(b), cols(h)] = dot(probs, v_ref[rows(b), cols(h)], ((1,), (0,)))
        return carry

    lax.fori_loop(0, heads // per, intra, 0)

    def prefix(c, carry):
        h = r * hq + c
        for t in (1, 2, 3):
            p1_arrival(c, t).wait_recv()
        decay = power(h, 2.0 * BLOCK)
        total = jnp.zeros((HD, HD), F32)
        reach = jnp.ones((1, HD), F32)
        pre[c, 0, 0:HD] = total
        pre[c, 0, HD:HD + 8] = jnp.ones((8, HD), F32)
        for s in range(GROUP):
            step = p1[c, s, HD:HD + 1] * decay
            total = step * total + p1[c, s, 0:HD]
            reach = reach * step
            pre[c, s + 1, 0:HD] = total
            pre[c, s + 1, HD:HD + 8] = jnp.broadcast_to(reach, (8, HD))
        return carry

    lax.fori_loop(0, hq, prefix, 0)

    def ch_copy(c):
        return remote(chain_out.at[c], chain_in.at[c], ch_send.at[c], ch_recv.at[c], p + GROUP, me)

    def p3_copy(c, t):
        to = (r + t) % GROUP
        return remote(p3out.at[c, t - 1], p3.at[c, r], p3_send.at[c, t - 1], p3_recv.at[c, r], base + to, me)

    def p3_arrival(c, t):
        src = (r + t) % GROUP
        return remote(p3out.at[c, t - 1], p3.at[c, src], p3_send.at[c, t - 1], p3_recv.at[c, src], base + src, me)

    def onward(c, carry):
        @pl.when(g == 0)
        def _():
            chain_in[c] = jnp.zeros((HD, HD), F32)

        @pl.when(g > 0)
        def _():
            remote(chain_out.at[c], chain_in.at[c], ch_send.at[c], ch_recv.at[c], p - GROUP, me).wait_recv()

        @pl.when(g < zs - 1)
        def _():
            chain_out[c] = pre[c, GROUP, HD:HD + 1] * chain_in[c] + pre[c, GROUP, 0:HD]
            ch_copy(c).start()

        incoming = chain_in[c]
        for t in (1, 2, 3):
            to = (r + t) % GROUP
            p3out[c, t - 1] = pre[c, to, HD:HD + 1] * incoming + pre[c, to, 0:HD]
            p3_copy(c, t).start()
        p3[c, r] = pre[c, r, HD:HD + 1] * incoming + pre[c, r, 0:HD]
        return carry

    lax.fori_loop(0, hq, onward, 0)

    ssq[...] = jnp.zeros_like(ssq)

    def inter(c, carry):
        for t in range(GROUP):
            src = (r + t) % GROUP
            h = src * hq + c
            if t:
                p3_arrival(c, t).wait_recv()
            state = p3[c, src]
            decay = jnp.exp(-rate_ref[h] * (place_f + 1.0))
            for b in range(2):
                if b:
                    state = (flag[0] * power(h, float(BLOCK))) * state + u0[h]
                high = state.astype(BF16)
                low = (state - high.astype(F32)).astype(BF16)
                queries = q_ref[rows(b), cols(h)]
                got = dot(
                    jnp.concatenate([queries, queries], axis=1),
                    jnp.concatenate([high, low], axis=0),
                    ((1,), (0,)),
                )
                got = jnp.where(place < start[b], got * decay, 0.0)
                new = att[rows(b), cols(h)] + got
                att[rows(b), cols(h)] = new
                ssq[rows(b)] = ssq[rows(b)] + new * new
        return carry

    lax.fori_loop(0, hq, inter, 0)

    def sq_copy(t):
        return remote(ssq, ssq_in.at[t - 1], sq_send.at[t - 1], sq_recv.at[t - 1], p, (me + t) % hn)

    for t in range(1, hn):
        sq_copy(t).start()
    for t in range(1, hn):
        sq_copy(t).wait_recv()

    def normed(start_row):
        at = pl.ds(start_row, CROWS)
        squares = ssq[at]
        for t in range(1, hn):
            squares = squares + ssq_in[t - 1, at]
        totals = jnp.sum(squares, axis=1, keepdims=True)
        scaling = lax.rsqrt(totals / (width * hn) + EPSILON)
        return (att[at, :] * scaling * gain_ref[...]).astype(BF16)

    def part(i):
        return pl.ds(i * CROWS, CROWS)

    def ha_copy(i, ctx):
        return remote(halo_out.at[part(i)], halo_in.at[part(i)], ha_send.at[i], ha_recv.at[i], ctx, me)

    for i in range(CHUNKS):
        halo_out[part(i)] = normed(i * CROWS)

        @pl.when(p > 0)
        def _():
            ha_copy(i, p - 1).start()

    here = plan_ref[p]
    there = jnp.where(p < n - 1, plan_ref[jnp.minimum(p + 1, n - 1)], 0)

    for i in range(CHUNKS):
        own1[part(i)] = normed(BLOCK + i * CROWS)
        out_ref[part(i)] = jnp.where(here == 0, halo_out[part(i)], own1[part(i)])

    @pl.when(p == n - 1)
    def _():
        halo_in[...] = jnp.zeros_like(halo_in)

    for i in range(CHUNKS):
        @pl.when(p < n - 1)
        def _():
            ha_copy(i, p + 1).wait_recv()

        following = jnp.where(there == 1, halo_in[part(i)], jnp.zeros((), BF16))
        out_ref[pl.ds(BLOCK + i * CROWS, CROWS)] = jnp.where(here == 0, own1[part(i)], following)
        out_ref[pl.ds(2 * BLOCK + i * CROWS, CROWS)] = jnp.where(
            here == 0, following, jnp.zeros((), BF16)
        )

    def drain(c, carry):
        for t in (1, 2, 3):
            p1_copy(c, t).wait_send()
            p3_copy(c, t).wait_send()

        @pl.when(g < zs - 1)
        def _():
            ch_copy(c).wait_send()

        return carry

    lax.fori_loop(0, hq, drain, 0)
    for t in range(1, hn):
        sq_copy(t).wait_send()
    for i in range(CHUNKS):
        @pl.when(p > 0)
        def _():
            ha_copy(i, p - 1).wait_send()


def body(n, hn, queries, keys, values, doc_start, decay_rate, gain, plan_offset):
    width = queries.shape[1]
    heads = width // HD
    hq = heads // GROUP
    vmem = pl.BlockSpec(memory_space=pltpu.VMEM)
    smem = pl.BlockSpec(memory_space=pltpu.SMEM)
    dma = pltpu.SemaphoreType.DMA
    partners = max(hn - 1, 1)
    return pl.pallas_call(
        functools.partial(kernel, n, hn, heads, width),
        out_shape=jax.ShapeDtypeStruct((3 * BLOCK, width), BF16),
        in_specs=[smem, smem, smem, vmem, vmem, vmem, vmem],
        out_specs=vmem,
        scratch_shapes=[
            pltpu.VMEM((2 * BLOCK, width), F32),
            pltpu.VMEM((heads, HD, HD), F32),
            pltpu.VMEM((2, BLOCK, BLOCK), F32),
            pltpu.VMEM((BLOCK, BLOCK), F32),
            pltpu.VMEM((hq, GROUP - 1, HD + 8, HD), F32),
            pltpu.VMEM((hq, GROUP, HD + 8, HD), F32),
            pltpu.VMEM((hq, GROUP + 1, HD + 8, HD), F32),
            pltpu.VMEM((hq, HD, HD), F32),
            pltpu.VMEM((hq, HD, HD), F32),
            pltpu.VMEM((hq, GROUP - 1, HD, HD), F32),
            pltpu.VMEM((hq, GROUP, HD, HD), F32),
            pltpu.VMEM((2 * BLOCK, HD), F32),
            pltpu.VMEM((partners, 2 * BLOCK, HD), F32),
            pltpu.VMEM((BLOCK, width), BF16),
            pltpu.VMEM((BLOCK, width), BF16),
            pltpu.VMEM((BLOCK, width), BF16),
            dma((hq, GROUP - 1)),
            dma((hq, GROUP)),
            dma((hq,)),
            dma((hq,)),
            dma((hq, GROUP - 1)),
            dma((hq, GROUP)),
            dma((partners,)),
            dma((partners,)),
            dma((CHUNKS,)),
            dma((CHUNKS,)),
        ],
        compiler_params=pltpu.CompilerParams(
            collective_id=0, has_side_effects=True, vmem_limit_bytes=48 * 1024 * 1024
        ),
    )(doc_start, decay_rate, plan_offset, queries, keys, values, gain.reshape(1, width))


def solution(mesh):
    in_specs = (
        P("ctx", "head"),
        P("ctx", "head"),
        P("ctx", "head"),
        P("ctx"),
        P("head"),
        P("head"),
        P(),
    )
    return jax.shard_map(
        functools.partial(body, mesh.shape["ctx"], mesh.shape["head"]),
        mesh=mesh,
        in_specs=in_specs,
        out_specs=P("ctx", "head"),
        check_vma=False,
    )
```

```python
import functools

import jax
import jax.numpy as jnp
from jax import lax
from jax.experimental import pallas as pl
from jax.experimental.pallas import tpu as pltpu
from jax.sharding import PartitionSpec as P

HD = 128
BLOCK = 256
GROUP = 4
EPSILON = 1e-06
F32 = jnp.float32
BF16 = jnp.bfloat16
CHUNKS = 4
CROWS = BLOCK // CHUNKS


def dot(a, b, dims):
    return lax.dot_general(a, b, (dims, ((), ())), preferred_element_type=F32)


def kernel(
    n, hn, heads, width,
    start_ref, rate_ref, gain_ref, q_hbm, k_hbm, v_hbm,
    out_ref,
    q_ref, k_ref, v_ref,
    att, u0, mask, dist, sbuf, p1, pre, chain_in, chain_out, p3out, p3,
    ssq, ssq_in, own,
    p1_send, p1_recv, ch_send, ch_recv, p3_send, p3_recv, sq_send, sq_recv, ha_send, ha_recv, in_sem, out_sem,
):
    hq = heads // GROUP
    zs = n // GROUP
    p = lax.axis_index("ctx")
    me = lax.axis_index("head")
    g = p // GROUP
    r = p % GROUP
    base = g * GROUP

    loads = [
        pltpu.make_async_copy(source, here, in_sem.at[i])
        for i, (source, here) in enumerate(((k_hbm, k_ref), (v_hbm, v_ref), (q_hbm, q_ref)))
    ]
    for load in loads:
        load.start()

    barrier = pltpu.get_barrier_semaphore()

    def greet(ctx, head):
        pl.semaphore_signal(
            barrier, inc=1, device_id=(ctx, head), device_id_type=pl.DeviceIdType.MESH
        )

    for t in range(1, GROUP):
        greet(base + (r + t) % GROUP, me)
    for t in range(1, hn):
        greet(p, (me + t) % hn)
    pl.when(g > 0)(lambda: greet(p - GROUP, me))
    pl.when(g < zs - 1)(lambda: greet(p + GROUP, me))
    pl.when(p > 0)(lambda: greet(p - 1, me))
    pl.when(p < n - 1)(lambda: greet(p + 1, me))

    start = [start_ref[0], start_ref[1]]
    flag = [jnp.where(s == BLOCK, 1.0, 0.0).astype(F32) for s in start]

    def cols(h):
        return pl.ds(pl.multiple_of(h * HD, HD), HD)

    def rows(b):
        return pl.ds(b * BLOCK, BLOCK)

    def power(h, count):
        return jnp.exp(jnp.full((1, HD), -rate_ref[h] * count, F32))

    def remote(src, dst, send, recv, ctx, head):
        return pltpu.make_async_remote_copy(
            src_ref=src, dst_ref=dst, send_sem=send, recv_sem=recv,
            device_id=(ctx, head), device_id_type=pl.DeviceIdType.MESH,
        )

    place = lax.broadcasted_iota(jnp.int32, (BLOCK, HD), 0)
    place_f = place.astype(F32)

    def shard_state(h):
        decay = jnp.exp(-rate_ref[h] * (BLOCK - 1 - place_f))
        parts = []
        for b in range(2):
            keys = k_ref[rows(b), cols(h)].astype(F32) * decay
            weighted = jnp.where(place >= start[b], keys, 0.0).astype(BF16)
            parts.append(dot(weighted, v_ref[rows(b), cols(h)], ((0,), (0,))))
        u0[h] = parts[0]
        return (flag[1] * power(h, float(BLOCK))) * parts[0] + parts[1]

    both = jnp.full((8, HD), flag[0] * flag[1], F32)

    def p1_copy(c, t):
        to = (r + t) % GROUP
        return remote(sbuf.at[c, t - 1], p1.at[c, r], p1_send.at[c, t - 1], p1_recv.at[c, r], base + to, me)

    def p1_arrival(c, t):
        src = (r + t) % GROUP
        return remote(sbuf.at[c, t - 1], p1.at[c, src], p1_send.at[c, t - 1], p1_recv.at[c, src], base + src, me)

    def first(c, carry):
        for t in (1, 2, 3):
            to = (r + t) % GROUP
            sbuf[c, t - 1, 0:HD] = shard_state(to * hq + c)
            sbuf[c, t - 1, HD:HD + 8] = both
        p1[c, r, 0:HD] = shard_state(r * hq + c)
        p1[c, r, HD:HD + 8] = both

        @pl.when(c == 0)
        def _():
            expected = GROUP - 1 + hn - 1
            expected = expected + jnp.where(g > 0, 1, 0) + jnp.where(g < zs - 1, 1, 0)
            expected = expected + jnp.where(p > 0, 1, 0) + jnp.where(p < n - 1, 1, 0)
            pl.semaphore_wait(barrier, expected)

        for t in (1, 2, 3):
            p1_copy(c, t).start()
        return carry

    loads[0].wait()
    loads[1].wait()
    lax.fori_loop(0, hq, first, 0)

    i_at = lax.broadcasted_iota(jnp.int32, (BLOCK, BLOCK), 0)
    j_at = lax.broadcasted_iota(jnp.int32, (BLOCK, BLOCK), 1)
    apart = i_at - j_at
    dist[...] = jnp.maximum(apart, 0).astype(F32)
    for b in range(2):
        blocked = (j_at < start[b]) & (start[b] <= i_at)
        mask[b] = jnp.where(blocked, 0.0, jnp.where(apart >= 0, 1.0, 0.0))

    def intra(step):
        for s in range(GROUP):
            h = step * GROUP + s
            weights = jnp.exp(-rate_ref[h] * dist[...])
            for b in range(2):
                scores = dot(q_ref[rows(b), cols(h)], k_ref[rows(b), cols(h)], ((1,), (1,)))
                probs = (scores * weights * mask[b]).astype(BF16)
                att[rows(b), cols(h)] = dot(probs, v_ref[rows(b), cols(h)], ((1,), (0,)))

    def prefix(c):
        h = r * hq + c
        for t in (1, 2, 3):
            p1_arrival(c, t).wait_recv()
        decay = power(h, 2.0 * BLOCK)
        total = jnp.zeros((HD, HD), F32)
        reach = jnp.ones((1, HD), F32)
        pre[c, 0, 0:HD] = total
        pre[c, 0, HD:HD + 8] = jnp.ones((8, HD), F32)
        for s in range(GROUP):
            step = p1[c, s, HD:HD + 1] * decay
            total = step * total + p1[c, s, 0:HD]
            reach = reach * step
            pre[c, s + 1, 0:HD] = total
            pre[c, s + 1, HD:HD + 8] = jnp.broadcast_to(reach, (8, HD))

    def ch_copy(c):
        return remote(chain_out.at[c], chain_in.at[c], ch_send.at[c], ch_recv.at[c], p + GROUP, me)

    def p3_copy(c, t):
        to = (r + t) % GROUP
        return remote(p3out.at[c, t - 1], p3.at[c, r], p3_send.at[c, t - 1], p3_recv.at[c, r], base + to, me)

    def p3_arrival(c, t):
        src = (r + t) % GROUP
        return remote(p3out.at[c, t - 1], p3.at[c, src], p3_send.at[c, t - 1], p3_recv.at[c, src], base + src, me)

    def onward(c, carry):
        intra(c)
        prefix(c)

        @pl.when(g == 0)
        def _():
            chain_in[c] = jnp.zeros((HD, HD), F32)

        @pl.when(g > 0)
        def _():
            remote(chain_out.at[c], chain_in.at[c], ch_send.at[c], ch_recv.at[c], p - GROUP, me).wait_recv()

        @pl.when(g < zs - 1)
        def _():
            chain_out[c] = pre[c, GROUP, HD:HD + 1] * chain_in[c] + pre[c, GROUP, 0:HD]
            ch_copy(c).start()

        incoming = chain_in[c]
        for t in (1, 2, 3):
            to = (r + t) % GROUP
            p3out[c, t - 1] = pre[c, to, HD:HD + 1] * incoming + pre[c, to, 0:HD]
            p3_copy(c, t).start()
        p3[c, r] = pre[c, r, HD:HD + 1] * incoming + pre[c, r, 0:HD]
        return carry

    loads[2].wait()
    lax.fori_loop(0, hq, onward, 0)

    ssq[...] = jnp.zeros_like(ssq)

    def inter(c, carry):
        for t in range(GROUP):
            src = (r + t) % GROUP
            h = src * hq + c
            if t:
                p3_arrival(c, t).wait_recv()
            state = p3[c, src]
            decay = jnp.exp(-rate_ref[h] * (place_f + 1.0))
            for b in range(2):
                if b:
                    state = (flag[0] * power(h, float(BLOCK))) * state + u0[h]
                high = state.astype(BF16)
                low = (state - high.astype(F32)).astype(BF16)
                queries = q_ref[rows(b), cols(h)]
                got = dot(
                    jnp.concatenate([queries, queries], axis=1),
                    jnp.concatenate([high, low], axis=0),
                    ((1,), (0,)),
                )
                got = jnp.where(place < start[b], got * decay, 0.0)
                new = att[rows(b), cols(h)] + got
                att[rows(b), cols(h)] = new
                ssq[rows(b)] = ssq[rows(b)] + new * new
        return carry

    lax.fori_loop(0, hq, inter, 0)

    def sq_copy(t):
        return remote(ssq, ssq_in.at[t - 1], sq_send.at[t - 1], sq_recv.at[t - 1], p, (me + t) % hn)

    for t in range(1, hn):
        sq_copy(t).start()
    for t in range(1, hn):
        sq_copy(t).wait_recv()

    def normed(start_row):
        at = pl.ds(start_row, CROWS)
        squares = ssq[at]
        for t in range(1, hn):
            squares = squares + ssq_in[t - 1, at]
        totals = jnp.sum(squares, axis=1, keepdims=True)
        scaling = lax.rsqrt(totals / (width * hn) + EPSILON)
        return (att[at, :] * scaling * gain_ref[...]).astype(BF16)

    def part(i):
        return pl.ds(i * CROWS, CROWS)

    def ha_copy(i, ctx):
        return remote(
            own.at[part(i)], out_ref.at[pl.ds(2 * BLOCK + i * CROWS, CROWS)],
            ha_send.at[i], ha_recv.at[i], ctx, me,
        )

    def keep(i):
        return pltpu.make_async_copy(own.at[part(i)], out_ref.at[part(i)], out_sem.at[i])

    for i in range(2 * CHUNKS):
        own[part(i)] = normed(i * CROWS)
        if i < CHUNKS:
            @pl.when(p > 0)
            def _():
                ha_copy(i, p - 1).start()

        keep(i).start()

    def drain(c, carry):
        for t in (1, 2, 3):
            p1_copy(c, t).wait_send()
            p3_copy(c, t).wait_send()

        @pl.when(g < zs - 1)
        def _():
            ch_copy(c).wait_send()

        return carry

    lax.fori_loop(0, hq, drain, 0)
    for t in range(1, hn):
        sq_copy(t).wait_send()
    for i in range(2 * CHUNKS):
        keep(i).wait()
    for i in range(CHUNKS):
        @pl.when(p > 0)
        def _():
            ha_copy(i, p - 1).wait_send()

        @pl.when(p < n - 1)
        def _():
            ha_copy(i, p + 1).wait_recv()


def placed(n, plan_ref, mine_ref, out_ref, slots, in_sem, out_sem):
    p = lax.axis_index("ctx")
    here = plan_ref[p]
    there = jnp.where(p < n - 1, plan_ref[jnp.minimum(p + 1, n - 1)], 0)
    length = 2 + there - here

    def fetch(i):
        row = pl.multiple_of(jnp.minimum(here + i, 2) * BLOCK, BLOCK)
        return pltpu.make_async_copy(mine_ref.at[pl.ds(row, BLOCK)], slots.at[i], in_sem.at[i])

    def put(i):
        return pltpu.make_async_copy(slots.at[i], out_ref.at[pl.ds(i * BLOCK, BLOCK)], out_sem.at[i])

    for i in range(3):
        pl.when(i < length)(lambda: fetch(i).start())
    for i in (2, 1, 0):
        @pl.when(i >= length)
        def _():
            slots[i] = jnp.zeros(slots.shape[1:], BF16)
            put(i).start()
    for i in range(3):
        @pl.when(i < length)
        def _():
            fetch(i).wait()
            put(i).start()
    for i in range(3):
        put(i).wait()


def place(mine, offset, n):
    return pl.pallas_call(
        functools.partial(placed, n),
        out_shape=jax.ShapeDtypeStruct(mine.shape, BF16),
        in_specs=[pl.BlockSpec(memory_space=pltpu.SMEM), pl.BlockSpec(memory_space=pl.ANY)],
        out_specs=pl.BlockSpec(memory_space=pl.ANY),
        scratch_shapes=[
            pltpu.VMEM((3, BLOCK, mine.shape[1]), BF16),
            pltpu.SemaphoreType.DMA((3,)),
            pltpu.SemaphoreType.DMA((3,)),
        ],
        compiler_params=pltpu.CompilerParams(vmem_limit_bytes=60 * 1024 * 1024),
    )(offset, mine)


def body(n, hn, queries, keys, values, doc_start, decay_rate, gain, plan_offset):
    width = queries.shape[1]
    heads = width // HD
    hq = heads // GROUP
    vmem = pl.BlockSpec(memory_space=pltpu.VMEM)
    hbm = pl.BlockSpec(memory_space=pl.ANY)
    smem = pl.BlockSpec(memory_space=pltpu.SMEM)
    dma = pltpu.SemaphoreType.DMA
    partners = max(hn - 1, 1)
    mine = pl.pallas_call(
        functools.partial(kernel, n, hn, heads, width),
        out_shape=jax.ShapeDtypeStruct((3 * BLOCK, width), BF16),
        in_specs=[smem, smem, vmem, hbm, hbm, hbm],
        out_specs=hbm,
        scratch_shapes=[
            pltpu.VMEM((2 * BLOCK, width), BF16),
            pltpu.VMEM((2 * BLOCK, width), BF16),
            pltpu.VMEM((2 * BLOCK, width), BF16),
            pltpu.VMEM((2 * BLOCK, width), F32),
            pltpu.VMEM((heads, HD, HD), F32),
            pltpu.VMEM((2, BLOCK, BLOCK), F32),
            pltpu.VMEM((BLOCK, BLOCK), F32),
            pltpu.VMEM((hq, GROUP - 1, HD + 8, HD), F32),
            pltpu.VMEM((hq, GROUP, HD + 8, HD), F32),
            pltpu.VMEM((hq, GROUP + 1, HD + 8, HD), F32),
            pltpu.VMEM((hq, HD, HD), F32),
            pltpu.VMEM((hq, HD, HD), F32),
            pltpu.VMEM((hq, GROUP - 1, HD, HD), F32),
            pltpu.VMEM((hq, GROUP, HD, HD), F32),
            pltpu.VMEM((2 * BLOCK, HD), F32),
            pltpu.VMEM((partners, 2 * BLOCK, HD), F32),
            pltpu.VMEM((2 * BLOCK, width), BF16),
            dma((hq, GROUP - 1)),
            dma((hq, GROUP)),
            dma((hq,)),
            dma((hq,)),
            dma((hq, GROUP - 1)),
            dma((hq, GROUP)),
            dma((partners,)),
            dma((partners,)),
            dma((CHUNKS,)),
            dma((CHUNKS,)),
            dma((3,)),
            dma((2 * CHUNKS,)),
        ],
        compiler_params=pltpu.CompilerParams(
            collective_id=0, has_side_effects=True, vmem_limit_bytes=60 * 1024 * 1024
        ),
    )(doc_start, decay_rate, gain.reshape(1, width), queries, keys, values)
    return place(mine, plan_offset, n)


def solution(mesh):
    in_specs = (
        P("ctx", "head"),
        P("ctx", "head"),
        P("ctx", "head"),
        P("ctx"),
        P("head"),
        P("head"),
        P(),
    )
    return jax.shard_map(
        functools.partial(body, mesh.shape["ctx"], mesh.shape["head"]),
        mesh=mesh,
        in_specs=in_specs,
        out_specs=P("ctx", "head"),
        check_vma=False,
    )
```

```python
import functools

import jax
import jax.numpy as jnp
from jax import lax
from jax.experimental import pallas as pl
from jax.experimental.pallas import tpu as pltpu
from jax.sharding import PartitionSpec as P

HD = 128
BLOCK = 256
GROUP = 4
EPSILON = 1e-06
F32 = jnp.float32
BF16 = jnp.bfloat16
CHUNKS = 4
LEVELS = 32000.0
TAIL = 16
CROWS = BLOCK // CHUNKS


def dot(a, b, dims):
    return lax.dot_general(a, b, (dims, ((), ())), preferred_element_type=F32)


def kernel(
    n, hn, heads, width,
    start_ref, rate_ref, gain_ref, q_hbm, k_hbm, v_hbm,
    out_ref,
    q_ref, k_ref, v_ref,
    att, u0, mask, dist, sbuf, p1, pre, chain_in, chain_out, p3out, p3,
    ssq, ssq_in, own,
    p1_send, p1_recv, ch_send, ch_recv, p3_send, p3_recv, sq_send, sq_recv, ha_send, ha_recv, in_sem, out_sem,
):
    hq = heads // GROUP
    zs = n // GROUP
    p = lax.axis_index("ctx")
    me = lax.axis_index("head")
    g = p // GROUP
    r = p % GROUP
    base = g * GROUP

    loads = [
        pltpu.make_async_copy(source, here, in_sem.at[i])
        for i, (source, here) in enumerate(((k_hbm, k_ref), (v_hbm, v_ref), (q_hbm, q_ref)))
    ]
    for load in loads:
        load.start()

    barrier = pltpu.get_barrier_semaphore()

    def greet(ctx, head):
        pl.semaphore_signal(
            barrier, inc=1, device_id=(ctx, head), device_id_type=pl.DeviceIdType.MESH
        )

    for t in range(1, GROUP):
        greet(base + (r + t) % GROUP, me)
    for t in range(1, hn):
        greet(p, (me + t) % hn)
    pl.when(g > 0)(lambda: greet(p - GROUP, me))
    pl.when(g < zs - 1)(lambda: greet(p + GROUP, me))
    pl.when(p > 0)(lambda: greet(p - 1, me))
    pl.when(p < n - 1)(lambda: greet(p + 1, me))

    start = [start_ref[0], start_ref[1]]
    flag = [jnp.where(s == BLOCK, 1.0, 0.0).astype(F32) for s in start]

    def cols(h):
        return pl.ds(pl.multiple_of(h * HD, HD), HD)

    def rows(b):
        return pl.ds(b * BLOCK, BLOCK)

    def power(h, count):
        return jnp.exp(jnp.full((1, HD), -rate_ref[h] * count, F32))

    def remote(src, dst, send, recv, ctx, head):
        return pltpu.make_async_remote_copy(
            src_ref=src, dst_ref=dst, send_sem=send, recv_sem=recv,
            device_id=(ctx, head), device_id_type=pl.DeviceIdType.MESH,
        )

    place = lax.broadcasted_iota(jnp.int32, (BLOCK, HD), 0)
    place_f = place.astype(F32)

    def shard_state(h):
        decay = jnp.exp(-rate_ref[h] * (BLOCK - 1 - place_f))
        parts = []
        for b in range(2):
            keys = k_ref[rows(b), cols(h)].astype(F32) * decay
            weighted = jnp.where(place >= start[b], keys, 0.0).astype(BF16)
            parts.append(dot(weighted, v_ref[rows(b), cols(h)], ((0,), (0,))))
        u0[h] = parts[0]
        return (flag[1] * power(h, float(BLOCK))) * parts[0] + parts[1]

    both = flag[0] * flag[1]

    def pack(ref, at, tile, bit):
        largest = jnp.max(jnp.abs(tile), axis=0, keepdims=True)
        power_of_two = jnp.ceil(jnp.log2(jnp.maximum(largest, 1e-30)))
        scaled = jnp.round(tile * (LEVELS * jnp.exp2(-power_of_two)))
        ref[(*at, pl.ds(0, HD))] = scaled.astype(jnp.int32).astype(jnp.int16)
        code = jnp.broadcast_to(2.0 * power_of_two + bit, (TAIL, HD))
        ref[(*at, pl.ds(HD, TAIL))] = code.astype(jnp.int32).astype(jnp.int16)

    def unpack(ref, at):
        code = ref[(*at, pl.ds(HD, TAIL))].astype(jnp.int32)[0:1]
        bit = (code & 1).astype(F32)
        power_of_two = (code >> 1).astype(F32)
        scale = jnp.exp2(power_of_two) * (1.0 / LEVELS)
        return ref[(*at, pl.ds(0, HD))].astype(jnp.int32).astype(F32) * scale, bit

    def p1_copy(c, t):
        to = (r + t) % GROUP
        return remote(sbuf.at[c, t - 1], p1.at[c, r], p1_send.at[c, t - 1], p1_recv.at[c, r], base + to, me)

    def p1_arrival(c, t):
        src = (r + t) % GROUP
        return remote(sbuf.at[c, t - 1], p1.at[c, src], p1_send.at[c, t - 1], p1_recv.at[c, src], base + src, me)

    def first(c, carry):
        for t in (1, 2, 3):
            to = (r + t) % GROUP
            pack(sbuf, (c, t - 1), shard_state(to * hq + c), both)
        pack(p1, (c, r), shard_state(r * hq + c), both)

        @pl.when(c == 0)
        def _():
            expected = GROUP - 1 + hn - 1
            expected = expected + jnp.where(g > 0, 1, 0) + jnp.where(g < zs - 1, 1, 0)
            expected = expected + jnp.where(p > 0, 1, 0) + jnp.where(p < n - 1, 1, 0)
            pl.semaphore_wait(barrier, expected)

        for t in (1, 2, 3):
            p1_copy(c, t).start()
        return carry

    loads[0].wait()
    loads[1].wait()
    lax.fori_loop(0, hq, first, 0)

    i_at = lax.broadcasted_iota(jnp.int32, (BLOCK, BLOCK), 0)
    j_at = lax.broadcasted_iota(jnp.int32, (BLOCK, BLOCK), 1)
    apart = i_at - j_at
    dist[...] = jnp.maximum(apart, 0).astype(F32)
    for b in range(2):
        blocked = (j_at < start[b]) & (start[b] <= i_at)
        mask[b] = jnp.where(blocked, 0.0, jnp.where(apart >= 0, 1.0, 0.0))

    def intra(step):
        for s in range(GROUP):
            h = step * GROUP + s
            weights = jnp.exp(-rate_ref[h] * dist[...])
            for b in range(2):
                scores = dot(q_ref[rows(b), cols(h)], k_ref[rows(b), cols(h)], ((1,), (1,)))
                probs = (scores * weights * mask[b]).astype(BF16)
                att[rows(b), cols(h)] = dot(probs, v_ref[rows(b), cols(h)], ((1,), (0,)))

    def prefix(c):
        h = r * hq + c
        for t in (1, 2, 3):
            p1_arrival(c, t).wait_recv()
        decay = power(h, 2.0 * BLOCK)
        total = jnp.zeros((HD, HD), F32)
        reach = jnp.ones((1, HD), F32)
        pre[c, 0, 0:HD] = total
        pre[c, 0, HD:HD + 8] = jnp.ones((8, HD), F32)
        for s in range(GROUP):
            part, bit = unpack(p1, (c, s))
            step = bit * decay
            total = step * total + part
            reach = reach * step
            pre[c, s + 1, 0:HD] = total
            pre[c, s + 1, HD:HD + 8] = jnp.broadcast_to(reach, (8, HD))

    def ch_copy(c):
        return remote(chain_out.at[c], chain_in.at[c], ch_send.at[c], ch_recv.at[c], p + GROUP, me)

    def p3_copy(c, t):
        to = (r + t) % GROUP
        return remote(p3out.at[c, t - 1], p3.at[c, r], p3_send.at[c, t - 1], p3_recv.at[c, r], base + to, me)

    def p3_arrival(c, t):
        src = (r + t) % GROUP
        return remote(p3out.at[c, t - 1], p3.at[c, src], p3_send.at[c, t - 1], p3_recv.at[c, src], base + src, me)

    def onward(c, carry):
        intra(c)
        prefix(c)

        @pl.when(g == 0)
        def _():
            chain_in[c] = jnp.zeros((HD, HD), F32)

        @pl.when(g > 0)
        def _():
            remote(chain_out.at[c], chain_in.at[c], ch_send.at[c], ch_recv.at[c], p - GROUP, me).wait_recv()

        @pl.when(g < zs - 1)
        def _():
            chain_out[c] = pre[c, GROUP, HD:HD + 1] * chain_in[c] + pre[c, GROUP, 0:HD]
            ch_copy(c).start()

        incoming = chain_in[c]
        for t in (1, 2, 3):
            to = (r + t) % GROUP
            pack(p3out, (c, t - 1), pre[c, to, HD:HD + 1] * incoming + pre[c, to, 0:HD], 0.0)
            p3_copy(c, t).start()
        pack(p3, (c, r), pre[c, r, HD:HD + 1] * incoming + pre[c, r, 0:HD], 0.0)
        return carry

    loads[2].wait()
    lax.fori_loop(0, hq, onward, 0)

    ssq[...] = jnp.zeros_like(ssq)

    def inter(c, carry):
        for t in range(GROUP):
            src = (r + t) % GROUP
            h = src * hq + c
            if t:
                p3_arrival(c, t).wait_recv()
            state, _ = unpack(p3, (c, src))
            decay = jnp.exp(-rate_ref[h] * (place_f + 1.0))
            for b in range(2):
                if b:
                    state = (flag[0] * power(h, float(BLOCK))) * state + u0[h]
                high = state.astype(BF16)
                low = (state - high.astype(F32)).astype(BF16)
                queries = q_ref[rows(b), cols(h)]
                got = dot(
                    jnp.concatenate([queries, queries], axis=1),
                    jnp.concatenate([high, low], axis=0),
                    ((1,), (0,)),
                )
                got = jnp.where(place < start[b], got * decay, 0.0)
                new = att[rows(b), cols(h)] + got
                att[rows(b), cols(h)] = new
                ssq[rows(b)] = ssq[rows(b)] + new * new
        return carry

    lax.fori_loop(0, hq, inter, 0)

    def sq_copy(t):
        return remote(ssq, ssq_in.at[t - 1], sq_send.at[t - 1], sq_recv.at[t - 1], p, (me + t) % hn)

    for t in range(1, hn):
        sq_copy(t).start()
    for t in range(1, hn):
        sq_copy(t).wait_recv()

    def normed(start_row):
        at = pl.ds(start_row, CROWS)
        squares = ssq[at]
        for t in range(1, hn):
            squares = squares + ssq_in[t - 1, at]
        totals = jnp.sum(squares, axis=1, keepdims=True)
        scaling = lax.rsqrt(totals / (width * hn) + EPSILON)
        return (att[at, :] * scaling * gain_ref[...]).astype(BF16)

    def part(i):
        return pl.ds(i * CROWS, CROWS)

    def ha_copy(i, ctx):
        return remote(
            own.at[part(i)], out_ref.at[pl.ds(2 * BLOCK + i * CROWS, CROWS)],
            ha_send.at[i], ha_recv.at[i], ctx, me,
        )

    def keep(i):
        return pltpu.make_async_copy(own.at[part(i)], out_ref.at[part(i)], out_sem.at[i])

    for i in range(2 * CHUNKS):
        own[part(i)] = normed(i * CROWS)
        if i < CHUNKS:
            @pl.when(p > 0)
            def _():
                ha_copy(i, p - 1).start()

        keep(i).start()

    def drain(c, carry):
        for t in (1, 2, 3):
            p1_copy(c, t).wait_send()
            p3_copy(c, t).wait_send()

        @pl.when(g < zs - 1)
        def _():
            ch_copy(c).wait_send()

        return carry

    lax.fori_loop(0, hq, drain, 0)
    for t in range(1, hn):
        sq_copy(t).wait_send()
    for i in range(2 * CHUNKS):
        keep(i).wait()
    for i in range(CHUNKS):
        @pl.when(p > 0)
        def _():
            ha_copy(i, p - 1).wait_send()

        @pl.when(p < n - 1)
        def _():
            ha_copy(i, p + 1).wait_recv()


def placed(n, plan_ref, mine_ref, out_ref, slots, in_sem, out_sem):
    p = lax.axis_index("ctx")
    here = plan_ref[p]
    there = jnp.where(p < n - 1, plan_ref[jnp.minimum(p + 1, n - 1)], 0)
    length = 2 + there - here

    def fetch(i):
        row = pl.multiple_of(jnp.minimum(here + i, 2) * BLOCK, BLOCK)
        return pltpu.make_async_copy(mine_ref.at[pl.ds(row, BLOCK)], slots.at[i], in_sem.at[i])

    def put(i):
        return pltpu.make_async_copy(slots.at[i], out_ref.at[pl.ds(i * BLOCK, BLOCK)], out_sem.at[i])

    for i in range(3):
        pl.when(i < length)(lambda: fetch(i).start())
    for i in (2, 1, 0):
        @pl.when(i >= length)
        def _():
            slots[i] = jnp.zeros(slots.shape[1:], BF16)
            put(i).start()
    for i in range(3):
        @pl.when(i < length)
        def _():
            fetch(i).wait()
            put(i).start()
    for i in range(3):
        put(i).wait()


def place(mine, offset, n):
    return pl.pallas_call(
        functools.partial(placed, n),
        out_shape=jax.ShapeDtypeStruct(mine.shape, BF16),
        in_specs=[pl.BlockSpec(memory_space=pltpu.SMEM), pl.BlockSpec(memory_space=pl.ANY)],
        out_specs=pl.BlockSpec(memory_space=pl.ANY),
        scratch_shapes=[
            pltpu.VMEM((3, BLOCK, mine.shape[1]), BF16),
            pltpu.SemaphoreType.DMA((3,)),
            pltpu.SemaphoreType.DMA((3,)),
        ],
        compiler_params=pltpu.CompilerParams(vmem_limit_bytes=60 * 1024 * 1024),
    )(offset, mine)


def body(n, hn, queries, keys, values, doc_start, decay_rate, gain, plan_offset):
    width = queries.shape[1]
    heads = width // HD
    hq = heads // GROUP
    vmem = pl.BlockSpec(memory_space=pltpu.VMEM)
    hbm = pl.BlockSpec(memory_space=pl.ANY)
    smem = pl.BlockSpec(memory_space=pltpu.SMEM)
    dma = pltpu.SemaphoreType.DMA
    partners = max(hn - 1, 1)
    mine = pl.pallas_call(
        functools.partial(kernel, n, hn, heads, width),
        out_shape=jax.ShapeDtypeStruct((3 * BLOCK, width), BF16),
        in_specs=[smem, smem, vmem, hbm, hbm, hbm],
        out_specs=hbm,
        scratch_shapes=[
            pltpu.VMEM((2 * BLOCK, width), BF16),
            pltpu.VMEM((2 * BLOCK, width), BF16),
            pltpu.VMEM((2 * BLOCK, width), BF16),
            pltpu.VMEM((2 * BLOCK, width), F32),
            pltpu.VMEM((heads, HD, HD), F32),
            pltpu.VMEM((2, BLOCK, BLOCK), F32),
            pltpu.VMEM((BLOCK, BLOCK), F32),
            pltpu.VMEM((hq, GROUP - 1, HD + TAIL, HD), jnp.int16),
            pltpu.VMEM((hq, GROUP, HD + TAIL, HD), jnp.int16),
            pltpu.VMEM((hq, GROUP + 1, HD + 8, HD), F32),
            pltpu.VMEM((hq, HD, HD), F32),
            pltpu.VMEM((hq, HD, HD), F32),
            pltpu.VMEM((hq, GROUP - 1, HD + TAIL, HD), jnp.int16),
            pltpu.VMEM((hq, GROUP, HD + TAIL, HD), jnp.int16),
            pltpu.VMEM((2 * BLOCK, HD), F32),
            pltpu.VMEM((partners, 2 * BLOCK, HD), F32),
            pltpu.VMEM((2 * BLOCK, width), BF16),
            dma((hq, GROUP - 1)),
            dma((hq, GROUP)),
            dma((hq,)),
            dma((hq,)),
            dma((hq, GROUP - 1)),
            dma((hq, GROUP)),
            dma((partners,)),
            dma((partners,)),
            dma((CHUNKS,)),
            dma((CHUNKS,)),
            dma((3,)),
            dma((2 * CHUNKS,)),
        ],
        compiler_params=pltpu.CompilerParams(
            collective_id=0, has_side_effects=True, vmem_limit_bytes=60 * 1024 * 1024
        ),
    )(doc_start, decay_rate, gain.reshape(1, width), queries, keys, values)
    return place(mine, plan_offset, n)


def solution(mesh):
    in_specs = (
        P("ctx", "head"),
        P("ctx", "head"),
        P("ctx", "head"),
        P("ctx"),
        P("head"),
        P("head"),
        P(),
    )
    return jax.shard_map(
        functools.partial(body, mesh.shape["ctx"], mesh.shape["head"]),
        mesh=mesh,
        in_specs=in_specs,
        out_specs=P("ctx", "head"),
        check_vma=False,
    )
```
